256 devices in a mesh: island: 2 (over core), tensor: 32 (over y, z_lo, x), fsdp: 4 (over z_hi).
Axes of the slice: x: 4, y: 4, z: 8 (z_hi: 4, z_lo: 2; z = z_hi * 2 + z_lo), core: 2. Of those that a mesh axis runs over, the one named last changes fastest.
Arguments:
- tokens: bfloat16 [8, 3584, 1792], P(('island', 'fsdp'), 'tensor'), may hold values from -6 to 6
- hidden_cot: bfloat16 [8, 3584, 8192], P(('island', 'fsdp'), None, 'tensor'), may hold values from -6 to 6
- inner_gate: float32 [2, 1792, 8192], P('island', 'fsdp', 'tensor'), may hold values from -6 to 6
- inner_up: float32 [2, 1792, 8192], P('island', 'fsdp', 'tensor'), may hold values from -6 to 6
- moment_gate: float32 [2, 1792, 8192], P('island', 'fsdp', 'tensor'), may hold values from -4 to 4
- moment_up: float32 [2, 1792, 8192], P('island', 'fsdp', 'tensor'), may hold values from -4 to 4
- second_gate: float32 [2, 1792, 8192], P('island', 'fsdp', 'tensor'), may hold values from 0.01 to 1
- second_up: float32 [2, 1792, 8192], P('island', 'fsdp', 'tensor'), may hold values from 0.01 to 1
- outer_gate: float32 [1792, 8192], P('fsdp', 'tensor'), may hold values from -6 to 6
- outer_up: float32 [1792, 8192], P('fsdp', 'tensor'), may hold values from -6 to 6
- velocity_gate: float32 [1792, 8192], P('fsdp', 'tensor'), may hold values from -4 to 4
- velocity_up: float32 [1792, 8192], P('fsdp', 'tensor'), may hold values from -4 to 4
- step_count: int32 [1], replicated, may hold values from 1 to 39
Outputs:
- new_outer_gate: float32 [1792, 8192], P('fsdp', 'tensor')
- new_outer_up: float32 [1792, 8192], P('fsdp', 'tensor')
- new_velocity_gate: float32 [1792, 8192], P('fsdp', 'tensor')
- new_velocity_up: float32 [1792, 8192], P('fsdp', 'tensor')
The draws below stay inside these ranges and needn't reach their ends.
All inputs are finite; a program needn't handle non-finite values.
Results may differ from the reference program's by a relative error of at most 0.00065.
Values may be sent and summed in bfloat16 or wider, within the bound.
No kernel may reach another device: no remote copies, remote signals or barrier semaphores. Data moves between devices by JAX's collectives and lax.ppermute only.
A program may use at most 192 MiB of HBM per device.

```python
import math
import jax
import jax.numpy as jnp

D = 1792
FF = 8192
GROUP_TOK = 3584
GROUPS = 8
TOKENS = 14336
ALL_TOKENS = 28672
N_ISLAND = 2


def block_scale(key, extent, shards, low, top_value):
    loudness = 1.0
    for position, parts in shards:
        heights = jax.random.uniform(jax.random.fold_in(jax.random.fold_in(key, 6), position), (parts,), jnp.float32, low / len(shards), top_value / len(shards))
        loudness = loudness * jnp.repeat(jnp.exp(heights), extent[position] // parts).reshape((-1,) + (1,) * (len(extent) - 1 - position))
    return loudness


def scatter_about(stream_key, extent, scale, reach, shards=(), dtype=jnp.bfloat16):
    drawn = jax.random.normal(stream_key, extent, jnp.float32) * scale
    if len(shards) > 0:
        drawn = block_scale(stream_key, extent, shards, -0.22, 0.18) * drawn
    return jnp.clip(drawn, min=-reach, max=reach).astype(dtype)


def setup_inputs(seed: int = 0) -> dict:
    streams_of = jax.random.split(jax.random.key(seed), 14)
    tokens = scatter_about(streams_of[0], (GROUPS, GROUP_TOK, D), 1.0, 6.0, ((0, 8), (1, 32)))
    hidden_cot = scatter_about(streams_of[1], (GROUPS, GROUP_TOK, FF), 1.0, 6.0, ((0, 8), (2, 32)))
    inner_gate = scatter_about(streams_of[2], (N_ISLAND, D, FF), 1.0, 6.0, ((0, 2), (1, 4), (2, 32)), jnp.float32)
    inner_up = scatter_about(streams_of[3], (N_ISLAND, D, FF), 1.0, 6.0, ((0, 2), (1, 4), (2, 32)), jnp.float32)
    moment_gate = scatter_about(streams_of[4], (N_ISLAND, D, FF), 0.5, 4.0, ((0, 2), (1, 4), (2, 32)), jnp.float32)
    moment_up = scatter_about(streams_of[5], (N_ISLAND, D, FF), 0.5, 4.0, ((0, 2), (1, 4), (2, 32)), jnp.float32)
    second_gate = jnp.clip(jnp.exp(math.log(1.0) - 4.6051702 * jax.random.uniform(streams_of[6], (N_ISLAND, D, FF), jnp.float32) ** block_scale(streams_of[6], (N_ISLAND, D, FF), ((0, 2), (1, 4), (2, 32)), -0.2, 0.2)), 0.01, 1.0)
    second_up = jnp.clip(jnp.exp(math.log(1.0) - 4.6051702 * jax.random.uniform(streams_of[7], (N_ISLAND, D, FF), jnp.float32) ** block_scale(streams_of[7], (N_ISLAND, D, FF), ((0, 2), (1, 4), (2, 32)), -0.2, 0.2)), 0.01, 1.0)
    outer_gate = scatter_about(streams_of[8], (D, FF), 1.0, 6.0, ((0, 4), (1, 32)), jnp.float32)
    outer_up = scatter_about(streams_of[9], (D, FF), 1.0, 6.0, ((0, 4), (1, 32)), jnp.float32)
    velocity_gate = scatter_about(streams_of[10], (D, FF), 0.5, 4.0, ((0, 4), (1, 32)), jnp.float32)
    velocity_up = scatter_about(streams_of[11], (D, FF), 0.5, 4.0, ((0, 4), (1, 32)), jnp.float32)
    step_count = jax.random.randint(streams_of[12], (1,), 1, 40).astype(jnp.int32)
    return {"tokens": tokens, "hidden_cot": hidden_cot, "inner_gate": inner_gate, "inner_up": inner_up, "moment_gate": moment_gate, "moment_up": moment_up, "second_gate": second_gate, "second_up": second_up, "outer_gate": outer_gate, "outer_up": outer_up, "velocity_gate": velocity_gate, "velocity_up": velocity_up, "step_count": step_count}


beta_first = 0.9
beta_second = 0.95
adam_eps = 1e-08
inner_rate = 0.03
decay_rate = 0.1
outer_momentum = 0.9
outer_rate = 0.7

def adamw_step(param, gradient, first, second, corr_first, corr_second):
    first_new = beta_first * first + (1.0 - beta_first) * gradient
    second_new = beta_second * second + (1.0 - beta_second) * gradient * gradient
    update = first_new / corr_first / (jnp.sqrt(second_new / corr_second) + adam_eps)
    return param - inner_rate * (update + decay_rate * param)

def reference(tokens, hidden_cot, inner_gate, inner_up, moment_gate, moment_up, second_gate, second_up, outer_gate, outer_up, velocity_gate, velocity_up, step_count):
    step_float = step_count[0].astype(jnp.float32)
    corr_first = 1.0 - jnp.exp(step_float * math.log(beta_first))
    corr_second = 1.0 - jnp.exp(step_float * math.log(beta_second))
    scale_in = D ** (-0.5)
    flat_x = tokens.reshape(ALL_TOKENS, D)
    flat_g = hidden_cot.reshape(ALL_TOKENS, FF)
    total_gate = jnp.zeros((D, FF), jnp.float32)
    total_up = jnp.zeros((D, FF), jnp.float32)
    for island in range(N_ISLAND):
        rows_x = flat_x[island * TOKENS:(island + 1) * TOKENS]
        rows_g = flat_g[island * TOKENS:(island + 1) * TOKENS].astype(jnp.float32)
        weight_gate = inner_gate[island].astype(jnp.bfloat16)
        weight_up = inner_up[island].astype(jnp.bfloat16)
        gate = jnp.dot(rows_x, weight_gate, preferred_element_type=jnp.float32) * scale_in
        upval = jnp.dot(rows_x, weight_up, preferred_element_type=jnp.float32) * scale_in
        sigmoid_gate = jax.nn.sigmoid(gate)
        dgate = (rows_g * upval * sigmoid_gate * (1.0 + gate * (1.0 - sigmoid_gate))).astype(jnp.bfloat16)
        dup = (rows_g * gate * sigmoid_gate).astype(jnp.bfloat16)
        grad_gate = jnp.dot(rows_x.T, dgate, preferred_element_type=jnp.float32) * scale_in
        grad_up = jnp.dot(rows_x.T, dup, preferred_element_type=jnp.float32) * scale_in
        new_gate = adamw_step(inner_gate[island], grad_gate, moment_gate[island], second_gate[island], corr_first, corr_second)
        new_up = adamw_step(inner_up[island], grad_up, moment_up[island], second_up[island], corr_first, corr_second)
        total_gate = total_gate + (outer_gate - new_gate)
        total_up = total_up + (outer_up - new_up)
    mean_gate = total_gate / float(N_ISLAND)
    mean_up = total_up / float(N_ISLAND)
    new_velocity_gate = outer_momentum * velocity_gate + mean_gate
    new_velocity_up = outer_momentum * velocity_up + mean_up
    new_outer_gate = outer_gate - outer_rate * (mean_gate + outer_momentum * new_velocity_gate)
    new_outer_up = outer_up - outer_rate * (mean_up + outer_momentum * new_velocity_up)
    return (new_outer_gate, new_outer_up, new_velocity_gate, new_velocity_up)
```

```python
import functools
import math

import jax
import jax.numpy as jnp
from jax import lax
from jax.experimental import pallas as pl
from jax.experimental.pallas import tpu as pltpu
from jax.sharding import PartitionSpec as P

beta_first = 0.9
beta_second = 0.95
adam_eps = 1e-08
inner_rate = 0.03
decay_rate = 0.1
outer_momentum = 0.9
outer_rate = 0.7

AXES = ("island", "tensor", "fsdp")
NX, NY, NL, NH = 4, 4, 2, 4


def route(target):
    pairs = []
    for c in range(2):
        for y in range(NY):
            for l in range(NL):
                for x in range(NX):
                    for h in range(NH):
                        dc, dy, dl, dx, dh = target(c, y, l, x, h)
                        src = (c * 32 + y * 8 + l * 4 + x) * 4 + h
                        dst = (dc * 32 + (dy % NY) * 8 + dl * 4 + dx % NX) * 4 + dh % NH
                        pairs.append((src, dst))
    return pairs


def send(block, target):
    return lax.ppermute(block, AXES, route(target))


def swap_hop(step):
    return lambda c, y, l, x, h: (l, y, c, x, h + step)


def high_hop(step):
    return lambda c, y, l, x, h: (c, y, l, x, h + step)


def first_hop(step):
    return lambda c, y, l, x, h: (c, y, l, x + step, h) if c == 0 else (c, y + step, l, x, h)


def second_hop(step):
    return lambda c, y, l, x, h: (c, y + step, l, x, h) if c == 0 else (c, y, l, x + step, h)


def core_hop(c, y, l, x, h):
    return (1 - c, y, l, x, h)


def block_kernel(layout, n_weights, final, scale, *refs):
    index_ref, refs = refs[0], refs[1:]
    weight_refs, refs = refs[:n_weights], refs[n_weights:]
    cot_ref, refs = refs[0], refs[1:]
    n_x = 1 + max(op for piece in layout for op, _, _ in piece)
    x_refs, refs = refs[:n_x], refs[n_x:]
    if final:
        given_ref, refs = refs[0], refs[1:]
        outs, refs = refs[:7], refs[7:]
        total, refs = refs[0], refs[1:]
    else:
        total, refs = refs[0], refs[1:]
    xbuf, gbuf, wbuf, pbuf, dbuf, xsem, gsem, wsem, tsem = refs
    n_pieces = len(layout)
    rows = xbuf.shape[1]
    feats = wbuf.shape[0]
    shard = feats // NH
    half = shard // 2
    cols = pbuf.shape[1] // 2
    per = gbuf.shape[1]
    high = index_ref[index_ref.shape[0] - 1]

    def fetch(piece, slot):
        for k in range(n_pieces):

            @pl.when(piece == k)
            def _(k=k):
                for op, first, count in layout[k]:
                    pltpu.make_async_copy(
                        x_refs[op], xbuf.at[slot, pl.ds(first, count)], xsem.at[slot]
                    ).start()

        for q in range(per):
            pltpu.make_async_copy(
                cot_ref.at[index_ref[piece * per + q]], gbuf.at[slot, q], gsem.at[slot]
            ).start()

    spots = ((0, 0), (1, 0), (2, 0), (2, 1), (3, 0))
    for ref, (ahead, part) in zip(weight_refs, spots):
        at = lax.rem(high + ahead, NH) * shard + part * half
        pltpu.make_async_copy(ref, wbuf.at[pl.ds(pl.multiple_of(at, 16), ref.shape[0])], wsem).start()
    fetch(0, 0)
    if final:
        pltpu.make_async_copy(given_ref, total, tsem).start()
    pltpu.make_async_copy(wbuf, wbuf, wsem).wait()

    def one(piece, carry):
        slot = lax.rem(piece, 2)

        @pl.when(piece + 1 < n_pieces)
        def _():
            fetch(piece + 1, 1 - slot)

        pltpu.make_async_copy(xbuf.at[slot], xbuf.at[slot], xsem.at[slot]).wait()
        pltpu.make_async_copy(gbuf.at[slot], gbuf.at[slot], gsem.at[slot]).wait()
        x = xbuf[slot]
        pbuf[...] = jnp.dot(x, wbuf[...], preferred_element_type=jnp.float32)
        tok = rows // per
        for q in range(per):
            at = pl.ds(q * tok, tok)
            gate = pbuf[at, :cols] * scale
            upval = pbuf[at, cols:] * scale
            cot = gbuf[slot, q].astype(jnp.float32)
            s = jax.nn.sigmoid(gate)
            cs = cot * s
            dbuf[at, :cols] = (cs * upval * (1.0 + gate * (1.0 - s))).astype(jnp.bfloat16)
            dbuf[at, cols:] = (cs * gate).astype(jnp.bfloat16)
        if final:

            @pl.when(piece == 0)
            def _():
                pltpu.make_async_copy(given_ref, total, tsem).wait()

        grad = lax.dot_general(
            x, dbuf[...], (((0,), (0,)), ((), ())), preferred_element_type=jnp.float32
        )
        if final:
            total[...] += grad
        else:

            @pl.when(piece == 0)
            def _():
                total[...] = grad

            @pl.when(piece > 0)
            def _():
                total[...] += grad

        return carry

    lax.fori_loop(0, n_pieces, one, 0)
    if final:

        def rounded(ahead, first, count):
            at = lax.rem(high + ahead, NH) * shard + first
            return (total[pl.ds(pl.multiple_of(at, 16), count), :] * scale).astype(jnp.bfloat16)

        opp_a, opp_b, up_a, up_b, down_a, down_b, own = outs
        opp_a[...] = rounded(2, 0, half)
        opp_b[...] = rounded(2, half, half)
        up_a[...] = rounded(1, 0, half)
        up_b[...] = rounded(1, half, half)
        down_a[...] = rounded(3, 0, half)
        down_b[...] = rounded(3, half, half)
        own[...] = rounded(0, 0, shard)


def blocks(index, weights, cot, xs, layout, given, scale):
    shard, wide = weights[0].shape
    feats = shard * NH
    per = 4
    rows = per * cot.shape[1]
    cols = wide // 2
    final = given is not None
    hbm = pl.BlockSpec(memory_space=pl.ANY)
    vmem = pl.BlockSpec(memory_space=pltpu.VMEM)
    operands = [index, *weights, cot, *xs]
    in_specs = [pl.BlockSpec(memory_space=pltpu.SMEM)] + [hbm] * (len(operands) - 1)
    scratch = []
    if final:
        operands.append(given)
        in_specs.append(hbm)
        half = jax.ShapeDtypeStruct((shard // 2, wide), jnp.bfloat16)
        out_shape = [half] * 6 + [jax.ShapeDtypeStruct((shard, wide), jnp.bfloat16)]
        out_specs = [vmem] * 7
        scratch.append(pltpu.VMEM((feats, wide), jnp.float32))
    else:
        out_shape = jax.ShapeDtypeStruct((feats, wide), jnp.float32)
        out_specs = vmem
    scratch += [
        pltpu.VMEM((2, rows, feats), jnp.bfloat16),
        pltpu.VMEM((2, per, cot.shape[1], cols), jnp.bfloat16),
        pltpu.VMEM((feats, wide), jnp.bfloat16),
        pltpu.VMEM((rows, wide), jnp.float32),
        pltpu.VMEM((rows, wide), jnp.bfloat16),
        pltpu.SemaphoreType.DMA((2,)),
        pltpu.SemaphoreType.DMA((2,)),
        pltpu.SemaphoreType.DMA,
        pltpu.SemaphoreType.DMA,
    ]
    flops = 4 * len(layout) * rows * feats * wide
    return pl.pallas_call(
        functools.partial(block_kernel, layout, len(weights), final, scale),
        out_shape=out_shape,
        in_specs=in_specs,
        out_specs=out_specs,
        scratch_shapes=scratch,
        cost_estimate=pl.CostEstimate(
            flops=flops, bytes_accessed=len(layout) * rows * feats * 2, transcendentals=0
        ),
        compiler_params=pltpu.CompilerParams(vmem_limit_bytes=40 * 1024 * 1024),
    )(*operands)


def shards(
    tokens,
    hidden_cot,
    inner_gate,
    inner_up,
    moment_gate,
    moment_up,
    second_gate,
    second_up,
    outer_gate,
    outer_up,
    velocity_gate,
    velocity_up,
    step_count,
):
    islands = float(lax.axis_size("island"))
    feats = tokens.shape[2]
    scale = feats ** (-0.5)
    core = lax.axis_index("island")
    place = lax.axis_index("tensor")
    high = lax.axis_index("fsdp")
    y, x = place // 8, place % 4
    tok = tokens.shape[1]
    shard, cols = inner_gate.shape[1:]
    half = shard // 2

    mine = send(tokens[0], swap_hop(0))
    local = jnp.concatenate([inner_gate[0], inner_up[0]], axis=1)
    local_low = local.astype(jnp.bfloat16)
    w_own = send(local_low, swap_hop(0))
    w_prev = send(local_low, swap_hop(1))
    w_next = send(local_low, swap_hop(-1))
    w_far_a = send(w_prev[:half], high_hop(1))
    w_far_b = send(w_next[half:], high_hop(-1))
    weights = [w_own, w_next, w_far_a, w_far_b, w_prev]

    before = send(mine, first_hop(1))
    after = send(mine, first_hop(-1))
    cut = tok // 2
    far_a = send(before[:cut], first_hop(1))
    far_b = send(after[cut:], first_hop(-1))
    line = jnp.concatenate([mine, before, after, far_a, far_b], axis=0)
    line_before = send(line, second_hop(1))
    line_after = send(line, second_hop(-1))
    cut = 2 * tok
    line_far_a = send(line_before[:cut], second_hop(1))
    line_far_b = send(line_after[cut:], second_hop(-1))
    line_o = send(line, core_hop)
    line_before_o = send(line_before, core_hop)
    line_after_o = send(line_after, core_hop)
    line_far_a_o = send(line_far_a, core_hop)
    line_far_b_o = send(line_far_b, core_hop)

    cot = send(hidden_cot[0], swap_hop(0)).reshape(-1, tok, cols)
    index = []
    for across in (0, -1, 1, 2):
        for lineage in (core, 1 - core):
            for along in (0, -1, 1, 2):
                sy = jnp.where(lineage == 0, y + across, y + along) % NY
                sx = jnp.where(lineage == 0, x + along, x + across) % NX
                index.append(sy * 8 + lineage * 4 + sx)
    index_early = jnp.stack(index[:24] + [high]).astype(jnp.int32)
    index_late = jnp.stack(index[24:] + [high]).astype(jnp.int32)
    rows = 4 * tok
    early = blocks(
        index_early,
        weights,
        cot,
        [line, line_o, line_before, line_before_o, line_after, line_after_o],
        [[(k, 0, rows)] for k in range(6)],
        None,
        scale,
    )
    opp_a, opp_b, up_a, up_b, down_a, down_b, own = blocks(
        index_late,
        weights,
        cot,
        [line_far_a, line_far_b, line_far_a_o, line_far_b_o],
        [[(0, 0, cut), (1, cut, cut)], [(2, 0, cut), (3, cut, cut)]],
        early,
        scale,
    )

    got_a = send(opp_a, high_hop(1))
    got_b = send(opp_b, high_hop(-1))
    from_prev_b = send(up_b, swap_hop(1))
    from_next_a = send(down_a, swap_hop(-1))
    from_own = send(own, swap_hop(0))

    def plus(a, b):
        return (a.astype(jnp.float32) + b.astype(jnp.float32)).astype(jnp.bfloat16)

    from_prev_a = send(plus(up_a, got_a), swap_hop(1))
    from_next_b = send(plus(down_b, got_b), swap_hop(-1))
    f32 = jnp.float32
    from_own = from_own.astype(f32)
    grad = jnp.concatenate(
        [
            from_own[:half] + from_prev_a.astype(f32) + from_next_a.astype(f32),
            from_own[half:] + from_prev_b.astype(f32) + from_next_b.astype(f32),
        ],
        axis=0,
    )

    step_float = step_count[0].astype(jnp.float32)
    corr_first = 1.0 - jnp.exp(step_float * math.log(beta_first))
    corr_second = 1.0 - jnp.exp(step_float * math.log(beta_second))

    def update(gradient, first, second):
        first_new = beta_first * first + (1.0 - beta_first) * gradient
        second_new = beta_second * second + (1.0 - beta_second) * gradient * gradient
        return first_new / corr_first / (jnp.sqrt(second_new / corr_second) + adam_eps)

    def rest(outer, param):
        return outer - (1.0 - inner_rate * decay_rate) * param

    rest_gate, rest_up = rest(outer_gate, inner_gate[0]), rest(outer_up, inner_up[0])
    rest_gate = rest_gate + send(rest_gate, core_hop)
    rest_up = rest_up + send(rest_up, core_hop)
    new_gate = update(grad[:, :cols], moment_gate[0], second_gate[0])
    new_up = update(grad[:, cols:], moment_up[0], second_up[0])
    new_gate = new_gate + send(new_gate, core_hop)
    new_up = new_up + send(new_up, core_hop)

    def apply(outer, velocity, fixed, change):
        mean_delta = (fixed + inner_rate * change) / islands
        velocity_new = outer_momentum * velocity + mean_delta
        return outer - outer_rate * (mean_delta + outer_momentum * velocity_new), velocity_new

    out_gate, vel_gate = apply(outer_gate, velocity_gate, rest_gate, new_gate)
    out_up, vel_up = apply(outer_up, velocity_up, rest_up, new_up)
    return (out_gate, out_up, vel_gate, vel_up)


def solution(mesh):
    state = P("island", "fsdp", "tensor")
    param = P("fsdp", "tensor")
    return jax.shard_map(
        shards,
        mesh=mesh,
        in_specs=(
            P(("island", "fsdp"), "tensor", None),
            P(("island", "fsdp"), None, "tensor"),
            *[state] * 6,
            *[param] * 4,
            P(),
        ),
        out_specs=(param,) * 4,
        check_vma=False,
    )
```

```python
import functools
import math

import jax
import jax.numpy as jnp
from jax import lax
from jax.experimental import pallas as pl
from jax.experimental.pallas import tpu as pltpu
from jax.sharding import Mesh
from jax.sharding import PartitionSpec as P

beta_first = 0.9
beta_second = 0.95
adam_eps = 1e-08
inner_rate = 0.03
decay_rate = 0.1
outer_momentum = 0.9
outer_rate = 0.7

AXES = ("core", "y", "low", "x", "high")
NY, NL, NX, NH = 4, 2, 4, 4
NZ = NL * NH


def route(target):
    pairs = []
    for c in range(2):
        for y in range(NY):
            for l in range(NL):
                for x in range(NX):
                    for h in range(NH):
                        dc, dy, dx, dz = target(c, y, x, h * NL + l)
                        dh, dl = dz % NZ // NL, dz % NL
                        src = (((c * NY + y) * NL + l) * NX + x) * NH + h
                        dst = (((dc * NY + dy % NY) * NL + dl) * NX + dx % NX) * NH + dh
                        pairs.append((src, dst))
    return pairs


def send(block, target):
    return lax.ppermute(block, AXES, route(target))


def first_hop(step):
    return lambda c, y, x, z: (c, y, x + step, z) if c == 0 else (c, y + step, x, z)


def second_hop(step):
    return lambda c, y, x, z: (c, y + step, x, z) if c == 0 else (c, y, x + step, z)


def z_hop(step):
    return lambda c, y, x, z: (c, y, x, z + step)


def low_hop(c, y, x, z):
    return c, y, x, z ^ 1


def core_hop(c, y, x, z):
    return 1 - c, y, x, z


def block_kernel(layout, side, scale, *refs):
    index_ref, own_ref, other_ref, refs = *refs[:3], refs[3:]
    weight_refs, refs = refs[: NZ + 1], refs[NZ + 1 :]
    n_x = 1 + max(op for piece in layout for op, _, _ in piece)
    x_refs, outs, refs = refs[:n_x], refs[n_x : n_x + NZ], refs[n_x + NZ :]
    xbuf, gbuf, wbuf, pbuf, dbuf, total, xsem, gsem, wsem = refs
    n_pieces = len(layout)
    rows = pbuf.shape[0]
    feats = wbuf.shape[0]
    shard = feats // NH
    pair = wbuf.shape[1] // 2
    cols = pair // 2
    tok = gbuf.shape[1]
    per = rows // tok
    spots = n_pieces * per

    first = 0
    for k, ref in zip((0, 1, 2, 3, 4, 4, 5, 6, 7), weight_refs):
        at = index_ref[2 * spots + k] * shard + first
        count = ref.shape[0]
        pltpu.make_async_copy(
            ref.at[:, pl.ds(side * pair, pair)],
            wbuf.at[pl.ds(pl.multiple_of(at, 16), count), pl.ds(k % 2 * pair, pair)],
            wsem,
        ).start()
        first = (first + count) % shard
    for k in range(n_pieces):
        for op, first, count in layout[k]:
            pltpu.make_async_copy(
                x_refs[op], xbuf.at[pl.ds(k * rows + first, count)], xsem.at[k]
            ).start()
        for spot in range(k * per, (k + 1) * per):
            for part, ref in enumerate((own_ref, other_ref)):
                pltpu.make_async_copy(
                    ref.at[index_ref[part * spots + spot], :, pl.ds(side * cols, cols)],
                    gbuf.at[spot, :, pl.ds(part * cols, cols)],
                    gsem.at[k],
                ).start()
    pltpu.make_async_copy(wbuf, wbuf, wsem).wait()

    def forward(k, carry):
        at = pl.ds(pl.multiple_of(k * rows, 16), rows)
        pltpu.make_async_copy(xbuf.at[at], xbuf.at[at], xsem.at[k]).wait()
        mine = gbuf.at[pl.ds(k * per, per)]
        pltpu.make_async_copy(mine, mine, gsem.at[k]).wait()
        pbuf[...] = jnp.dot(xbuf[at, :], wbuf[...], preferred_element_type=jnp.float32)
        for q in range(per):
            for part in range(2):
                first = part * pair
                gate = pbuf[pl.ds(q * tok, tok), first : first + cols] * scale
                upval = pbuf[pl.ds(q * tok, tok), first + cols : first + pair] * scale
                s = jax.nn.sigmoid(gate)
                cot = gbuf[k * per + q, :, part * cols : (part + 1) * cols]
                cs = cot.astype(jnp.float32) * s
                to = pl.ds(pl.multiple_of(k * rows + q * tok, 16), tok)
                dgate = cs * upval * (1.0 + gate * (1.0 - s))
                dbuf[to, first : first + cols] = dgate.astype(jnp.bfloat16)
                dbuf[to, first + cols : first + pair] = (cs * gate).astype(jnp.bfloat16)
        return carry

    lax.fori_loop(0, n_pieces, forward, 0)
    step = 256
    for j in range(0, feats, step):
        grad = lax.dot_general(
            xbuf[:, j : j + step],
            dbuf[...],
            (((0,), (0,)), ((), ())),
            preferred_element_type=jnp.float32,
        )
        for part in range(2):
            total[part, pl.ds(j, step), :] = grad[:, part * pair : (part + 1) * pair]
    for k, out in enumerate(outs):
        at = pl.multiple_of(index_ref[2 * spots + k] * shard, 16)
        out[...] = (total[k % 2, pl.ds(at, shard), :] * scale).astype(jnp.bfloat16)


def blocks(index, weights, own, other, xs, layout, side, scale):
    feats, pair = weights[0].shape[0] * NH, weights[0].shape[1] // 2
    tok = own.shape[1]
    per = 4
    rows = per * tok
    n = len(layout)
    hbm = pl.BlockSpec(memory_space=pl.ANY)
    vmem = pl.BlockSpec(memory_space=pltpu.VMEM)
    operands = [index, own, other, *weights, *xs]
    return pl.pallas_call(
        functools.partial(block_kernel, layout, side, scale),
        out_shape=[jax.ShapeDtypeStruct((feats // NH, pair), jnp.bfloat16)] * NZ,
        in_specs=[pl.BlockSpec(memory_space=pltpu.SMEM)] + [hbm] * (len(operands) - 1),
        out_specs=[vmem] * NZ,
        scratch_shapes=[
            pltpu.VMEM((n * rows, feats), jnp.bfloat16),
            pltpu.VMEM((n * per, tok, pair), jnp.bfloat16),
            pltpu.VMEM((feats, 2 * pair), jnp.bfloat16),
            pltpu.VMEM((rows, 2 * pair), jnp.float32),
            pltpu.VMEM((n * rows, 2 * pair), jnp.bfloat16),
            pltpu.VMEM((2, feats, pair), jnp.float32),
            pltpu.SemaphoreType.DMA((n,)),
            pltpu.SemaphoreType.DMA((n,)),
            pltpu.SemaphoreType.DMA,
        ],
        cost_estimate=pl.CostEstimate(
            flops=8 * n * rows * feats * pair, bytes_accessed=n * rows * feats * 2, transcendentals=0
        ),
        compiler_params=pltpu.CompilerParams(vmem_limit_bytes=36 * 1024 * 1024),
    )(*operands)


def plus(a, *others):
    total = a.astype(jnp.float32)
    for b in others:
        total = total + b.astype(jnp.float32)
    return total


def ring(parts):
    low = jnp.bfloat16
    half = parts[0].shape[0] // 2
    up = send(parts[4][:half], z_hop(1))
    down = send(parts[4][half:], z_hop(-1))
    up = jnp.concatenate([plus(parts[3][:half], up).astype(low), parts[3][half:]], axis=0)
    down = jnp.concatenate([parts[5][:half], plus(parts[5][half:], down).astype(low)], axis=0)
    up = send(up, z_hop(1))
    down = send(down, z_hop(-1))
    up = send(plus(parts[2], up).astype(low), z_hop(1))
    down = send(plus(parts[6], down).astype(low), z_hop(-1))
    up = send(plus(parts[1], up).astype(low), z_hop(1))
    down = send(plus(parts[7], down).astype(low), z_hop(-1))
    return plus(parts[0], up, down)


def shards(
    tokens,
    hidden_cot,
    inner_gate,
    inner_up,
    moment_gate,
    moment_up,
    second_gate,
    second_up,
    outer_gate,
    outer_up,
    velocity_gate,
    velocity_up,
    step_count,
):
    islands = float(lax.axis_size("core"))
    scale = tokens.shape[2] ** (-0.5)
    core, y, low, x, high = (lax.axis_index(name) for name in AXES)
    tok = tokens.shape[1]
    cols = inner_gate.shape[2]
    side = cols // 2
    sides = [slice(0, side), slice(side, cols)]

    local = jnp.concatenate(
        [part[0][:, at].astype(jnp.bfloat16) for at in sides for part in (inner_gate, inner_up)],
        axis=1,
    )
    down, up = [local], [local]
    for _ in range(NZ // 2 - 1):
        down.append(send(down[-1], z_hop(-1)))
        up.append(send(up[-1], z_hop(1)))
    cut = local.shape[0] // 2
    far = [send(up[-1][:cut], z_hop(1)), send(down[-1][cut:], z_hop(-1))]
    weights = [*down, *far, *up[:0:-1]]

    mine = tokens[0]
    before = send(mine, first_hop(1))
    after = send(mine, first_hop(-1))
    cut = tok // 2
    far_a = send(before[:cut], first_hop(1))
    far_b = send(after[cut:], first_hop(-1))
    line = jnp.concatenate([mine, before, after, far_a, far_b], axis=0)
    line_before = send(line, second_hop(1))
    line_after = send(line, second_hop(-1))
    cut = 2 * tok
    line_far_a = send(line_before[:cut], second_hop(1))
    line_far_b = send(line_after[cut:], second_hop(-1))

    own = hidden_cot[0].reshape(NY, NL, NX * tok, cols)
    other = lax.dynamic_index_in_dim(own, 1 - low, 1, keepdims=False)
    other = send(other, low_hop).reshape(NY * NX, tok, cols)
    own = own.reshape(NY * NL * NX, tok, cols)

    own_at, other_at = [], []
    for across in (0, -1, 1, 2):
        for along in (0, -1, 1, 2):
            sy = jnp.where(core == 0, y + across, y + along) % NY
            sx = jnp.where(core == 0, x + along, x + across) % NX
            own_at.append((sy * NL + low) * NX + sx)
            other_at.append(sy * NX + sx)
    z = high * NL + low
    feature_at = [(z + k) % NZ // NL for k in range(NZ)]
    index = jnp.stack(own_at + other_at + feature_at).astype(jnp.int32)
    rows = 4 * tok
    xs = [line, line_before, line_after, line_far_a, line_far_b]
    layout = [[(0, 0, rows)], [(1, 0, rows)], [(2, 0, rows)], [(3, 0, cut), (4, cut, cut)]]
    grads = [
        ring(blocks(index, weights, own, other, xs, layout, k, scale)) for k in range(2)
    ]

    step_float = step_count[0].astype(jnp.float32)
    corr_first = 1.0 - jnp.exp(step_float * math.log(beta_first))
    corr_second = 1.0 - jnp.exp(step_float * math.log(beta_second))

    def update(gradient, first, second):
        first_new = beta_first * first + (1.0 - beta_first) * gradient
        second_new = beta_second * second + (1.0 - beta_second) * gradient * gradient
        return first_new / corr_first / (jnp.sqrt(second_new / corr_second) + adam_eps)

    def rest(outer, param):
        return outer - (1.0 - inner_rate * decay_rate) * param

    resting = jnp.concatenate(
        [rest(outer_gate, inner_gate[0]), rest(outer_up, inner_up[0])], axis=1
    )
    resting = resting + send(resting, core_hop)

    changes = []
    for k, at in enumerate(sides):
        change = jnp.concatenate(
            [
                update(grads[k][:, :side], moment_gate[0][:, at], second_gate[0][:, at]),
                update(grads[k][:, side:], moment_up[0][:, at], second_up[0][:, at]),
            ],
            axis=1,
        )
        changes.append(change + send(change, core_hop))

    def apply(outer, velocity, fixed, change):
        mean_delta = (fixed + inner_rate * change) / islands
        velocity_new = outer_momentum * velocity + mean_delta
        return outer - outer_rate * (mean_delta + outer_momentum * velocity_new), velocity_new

    change_gate = jnp.concatenate([change[:, :side] for change in changes], axis=1)
    change_up = jnp.concatenate([change[:, side:] for change in changes], axis=1)
    out_gate, vel_gate = apply(outer_gate, velocity_gate, resting[:, :cols], change_gate)
    out_up, vel_up = apply(outer_up, velocity_up, resting[:, cols:], change_up)
    return (out_gate, out_up, vel_gate, vel_up)


def solution(mesh):
    split = Mesh(mesh.devices.reshape(2, NY, NL, NX, NH), AXES)
    tensor = ("y", "low", "x")
    state = P("core", "high", tensor)
    param = P("high", tensor)
    return jax.shard_map(
        shards,
        mesh=split,
        in_specs=(
            P(("core", "high"), tensor, None),
            P(("core", "high"), None, tensor),
            *[state] * 6,
            *[param] * 4,
            P(),
        ),
        out_specs=(param,) * 4,
        check_vma=False,
    )
```

```python
import functools
import math

import jax
import jax.numpy as jnp
from jax import lax
from jax.experimental import pallas as pl
from jax.experimental.pallas import tpu as pltpu
from jax.sharding import Mesh
from jax.sharding import PartitionSpec as P

beta_first = 0.9
beta_second = 0.95
adam_eps = 1e-08
inner_rate = 0.03
decay_rate = 0.1
outer_momentum = 0.9
outer_rate = 0.7

AXES = ("core", "y", "low", "x", "high")
NY, NL, NX, NH = 4, 2, 4, 4
NZ = NL * NH


def route(target):
    pairs = []
    for c in range(2):
        for y in range(NY):
            for l in range(NL):
                for x in range(NX):
                    for h in range(NH):
                        dc, dy, dx, dz = target(c, y, x, h * NL + l)
                        dh, dl = dz % NZ // NL, dz % NL
                        src = (((c * NY + y) * NL + l) * NX + x) * NH + h
                        dst = (((dc * NY + dy % NY) * NL + dl) * NX + dx % NX) * NH + dh
                        pairs.append((src, dst))
    return pairs


def send(block, target):
    return lax.ppermute(block, AXES, route(target))


def first_hop(step):
    return lambda c, y, x, z: (c, y, x + step, z) if c == 0 else (c, y + step, x, z)


def second_hop(step):
    return lambda c, y, x, z: (c, y + step, x, z) if c == 0 else (c, y, x + step, z)


def z_hop(step):
    return lambda c, y, x, z: (c, y, x, z + step)


def low_hop(c, y, x, z):
    return c, y, x, z ^ 1


def core_hop(c, y, x, z):
    return 1 - c, y, x, z


def block_kernel(layout, side, scale, given, final, *refs):
    index_ref, own_ref, other_ref, refs = *refs[:3], refs[3:]
    weight_refs, refs = refs[:NZ], refs[NZ:]
    n_x = 1 + max(op for piece in layout for op, _, _ in piece)
    x_refs, refs = refs[:n_x], refs[n_x:]
    if given:
        given_ref, refs = refs[0], refs[1:]
    if final:
        outs, refs = refs[:NZ], refs[NZ:]
    total, xbuf, gbuf, wbuf, pbuf, dbuf, xsem, gsem, wsem, tsem = refs
    n_pieces = len(layout)
    rows = pbuf.shape[0]
    feats = wbuf.shape[0]
    shard = feats // NH
    pair = wbuf.shape[1] // 2
    cols = pair // 2
    tok = gbuf.shape[1]
    per = rows // tok
    spots = n_pieces * per

    for k, ref in enumerate(weight_refs):
        at = pl.multiple_of(index_ref[2 * spots + k] * shard, 16)
        pltpu.make_async_copy(
            ref.at[:, pl.ds(side * pair, pair)],
            wbuf.at[pl.ds(at, shard), pl.ds(k % 2 * pair, pair)],
            wsem,
        ).start()
    for k in range(n_pieces):
        for op, first, count in layout[k]:
            pltpu.make_async_copy(
                x_refs[op], xbuf.at[pl.ds(k * rows + first, count)], xsem.at[k]
            ).start()
        for spot in range(k * per, (k + 1) * per):
            pltpu.make_async_copy(
                own_ref.at[index_ref[spot], :, pl.ds(side * cols, cols)],
                gbuf.at[spot, :, :cols],
                gsem.at[k],
            ).start()
            pltpu.make_async_copy(
                other_ref.at[index_ref[spots + spot]], gbuf.at[spot, :, cols:], gsem.at[k]
            ).start()
    if given:
        pltpu.make_async_copy(given_ref, total, tsem).start()
    pltpu.make_async_copy(wbuf, wbuf, wsem).wait()

    def forward(k, carry):
        at = pl.ds(pl.multiple_of(k * rows, 16), rows)
        pltpu.make_async_copy(xbuf.at[at], xbuf.at[at], xsem.at[k]).wait()
        mine = gbuf.at[pl.ds(k * per, per)]
        pltpu.make_async_copy(mine, mine, gsem.at[k]).wait()
        pbuf[...] = jnp.dot(xbuf[at, :], wbuf[...], preferred_element_type=jnp.float32)
        for q in range(per):
            for part in range(2):
                first = part * pair
                gate = pbuf[pl.ds(q * tok, tok), first : first + cols] * scale
                upval = pbuf[pl.ds(q * tok, tok), first + cols : first + pair] * scale
                s = jax.nn.sigmoid(gate)
                cot = gbuf[k * per + q, :, part * cols : (part + 1) * cols]
                cs = cot.astype(jnp.float32) * s
                to = pl.ds(pl.multiple_of(k * rows + q * tok, 16), tok)
                dgate = cs * upval * (1.0 + gate * (1.0 - s))
                dbuf[to, first : first + cols] = dgate.astype(jnp.bfloat16)
                dbuf[to, first + cols : first + pair] = (cs * gate).astype(jnp.bfloat16)
        return carry

    lax.fori_loop(0, n_pieces, forward, 0)
    if given:
        pltpu.make_async_copy(given_ref, total, tsem).wait()
    step = 256
    for j in range(0, feats, step):
        grad = lax.dot_general(
            xbuf[:, j : j + step],
            dbuf[...],
            (((0,), (0,)), ((), ())),
            preferred_element_type=jnp.float32,
        )
        for part in range(2):
            half = grad[:, part * pair : (part + 1) * pair]
            if given:
                half = half + total[part, pl.ds(j, step), :]
            total[part, pl.ds(j, step), :] = half
    if final:
        for k, out in enumerate(outs):
            at = pl.multiple_of(index_ref[2 * spots + k] * shard, 16)
            out[...] = (total[k % 2, pl.ds(at, shard), :] * scale).astype(jnp.bfloat16)


def blocks(index, weights, own, other, xs, layout, side, scale, given=None, final=True):
    feats, pair = weights[0].shape[0] * NH, weights[0].shape[1] // 2
    tok = own.shape[1]
    per = 4
    rows = per * tok
    n = len(layout)
    hbm = pl.BlockSpec(memory_space=pl.ANY)
    vmem = pl.BlockSpec(memory_space=pltpu.VMEM)
    operands = [index, own, other, *weights, *xs]
    if given is not None:
        operands.append(given)
    total = (2, feats, pair)
    if final:
        out_shape = [jax.ShapeDtypeStruct((feats // NH, pair), jnp.bfloat16)] * NZ
    else:
        out_shape = [jax.ShapeDtypeStruct(total, jnp.float32)]
    out = pl.pallas_call(
        functools.partial(block_kernel, layout, side, scale, given is not None, final),
        out_shape=out_shape,
        in_specs=[pl.BlockSpec(memory_space=pltpu.SMEM)] + [hbm] * (len(operands) - 1),
        out_specs=[vmem] * len(out_shape),
        scratch_shapes=([pltpu.VMEM(total, jnp.float32)] if final else [])
        + [
            pltpu.VMEM((n * rows, feats), jnp.bfloat16),
            pltpu.VMEM((n * per, tok, pair), jnp.bfloat16),
            pltpu.VMEM((feats, 2 * pair), jnp.bfloat16),
            pltpu.VMEM((rows, 2 * pair), jnp.float32),
            pltpu.VMEM((n * rows, 2 * pair), jnp.bfloat16),
            pltpu.SemaphoreType.DMA((n,)),
            pltpu.SemaphoreType.DMA((n,)),
            pltpu.SemaphoreType.DMA,
            pltpu.SemaphoreType.DMA,
        ],
        cost_estimate=pl.CostEstimate(
            flops=16 * n * rows * feats * pair, bytes_accessed=n * rows * feats * 2, transcendentals=0
        ),
        compiler_params=pltpu.CompilerParams(vmem_limit_bytes=36 * 1024 * 1024),
    )(*operands)
    return list(out) if final else out[0]


def pick_kernel(first_ref, second_ref, top, bottom, sems):
    cut = top.shape[0]
    copies = [
        pltpu.make_async_copy(first_ref.at[pl.ds(0, cut)], top, sems.at[0]),
        pltpu.make_async_copy(second_ref.at[pl.ds(cut, cut)], bottom, sems.at[1]),
    ]
    for copy in copies:
        copy.start()
    for copy in copies:
        copy.wait()


def pick(first, second):
    half = jax.ShapeDtypeStruct((first.shape[0] // 2, first.shape[1]), first.dtype)
    return pl.pallas_call(
        pick_kernel,
        out_shape=[half, half],
        in_specs=[pl.BlockSpec(memory_space=pl.ANY)] * 2,
        out_specs=[pl.BlockSpec(memory_space=pltpu.VMEM)] * 2,
        scratch_shapes=[pltpu.SemaphoreType.DMA((2,))],
        cost_estimate=pl.CostEstimate(
            flops=0, bytes_accessed=4 * first.size, transcendentals=0
        ),
        compiler_params=pltpu.CompilerParams(vmem_limit_bytes=36 * 1024 * 1024),
    )(first, second)


def tie(*arrays):
    return lax.optimization_barrier(arrays)


def rest(outer, param):
    return outer - (1.0 - inner_rate * decay_rate) * param


def plus(a, *others):
    total = a.astype(jnp.float32)
    for b in others:
        total = total + b.astype(jnp.float32)
    return total


def ring(parts):
    low = jnp.bfloat16
    half = parts[0].shape[0] // 2
    up = send(parts[4][:half], z_hop(1))
    down = send(parts[4][half:], z_hop(-1))
    up = jnp.concatenate([plus(parts[3][:half], up).astype(low), parts[3][half:]], axis=0)
    down = jnp.concatenate([parts[5][:half], plus(parts[5][half:], down).astype(low)], axis=0)
    up = send(up, z_hop(1))
    down = send(down, z_hop(-1))
    up = send(plus(parts[2], up).astype(low), z_hop(1))
    down = send(plus(parts[6], down).astype(low), z_hop(-1))
    up = send(plus(parts[1], up).astype(low), z_hop(1))
    down = send(plus(parts[7], down).astype(low), z_hop(-1))
    return plus(parts[0], up, down)


def shards(
    tokens,
    hidden_cot,
    inner_gate,
    inner_up,
    moment_gate,
    moment_up,
    second_gate,
    second_up,
    outer_gate,
    outer_up,
    velocity_gate,
    velocity_up,
    step_count,
):
    islands = float(lax.axis_size("core"))
    scale = tokens.shape[2] ** (-0.5)
    core, y, low, x, high = (lax.axis_index(name) for name in AXES)
    tok = tokens.shape[1]
    cols = inner_gate.shape[2]
    side = cols // 2
    sides = [slice(0, side), slice(side, cols)]

    local = jnp.concatenate(
        [part[0][:, at].astype(jnp.bfloat16) for at in sides for part in (inner_gate, inner_up)],
        axis=1,
    )
    resting = jnp.concatenate(
        [rest(outer_gate, inner_gate[0]), rest(outer_up, inner_up[0])], axis=1
    )
    own = hidden_cot[0].reshape(NY, NL, NX * tok, cols)
    other = lax.dynamic_index_in_dim(own, 1 - low, 1, keepdims=False)
    own = own.reshape(NY * NL * NX, tok, cols)
    mine = tokens[0]

    before = send(mine, first_hop(1))
    after = send(mine, first_hop(-1))
    far = send(mine, first_hop(2))
    up1 = send(local, z_hop(1))
    down1 = send(local, z_hop(-1))
    before, after, far, up1, down1 = tie(before, after, far, up1, down1)

    line = jnp.concatenate([mine, before, after, far], axis=0)
    line_before = send(line, second_hop(1))
    line_after = send(line, second_hop(-1))
    up2 = send(up1, z_hop(1))
    down2 = send(down1, z_hop(-1))
    up3 = send(up2, z_hop(1))
    down3 = send(down2, z_hop(-1))
    others = [
        send(other[..., at], low_hop).reshape(NY * NX, tok, side) for at in sides
    ]

    cut = 2 * tok
    line_before, line_after, others[0] = tie(line_before, line_after, others[0])
    top, bottom = pick(line_before, line_after)
    last_a = send(top, second_hop(1))
    last_b = send(bottom, second_hop(-1))
    opposite = send(jnp.where(low == 1, up3, down3), lambda c, y, x, z: (c, y, x, z - 1 + z % 2 * 2))
    weights = [local, down1, down2, down3, opposite, up3, up2, up1]

    own_at, other_at = [], []
    for across in (0, -1, 1, 2):
        for along in (0, -1, 1, 2):
            sy = jnp.where(core == 0, y + across, y + along) % NY
            sx = jnp.where(core == 0, x + along, x + across) % NX
            own_at.append((sy * NL + low) * NX + sx)
            other_at.append(sy * NX + sx)
    z = high * NL + low
    feature_at = [(z + k) % NZ // NL for k in range(NZ)]
    xs = [line, line_before, line_after, last_a, last_b]

    def run(side, bundles, given, final):
        spots = [spot for k in bundles for spot in range(4 * k, 4 * k + 4)]
        index = [own_at[k] for k in spots] + [other_at[k] for k in spots] + feature_at
        ops = [op for k in bundles for op in ((k,) if k < 3 else (3, 4))]
        layout = []
        for k in bundles:
            where = ops.index(k)
            layout.append([(where, 0, 4 * tok)] if k < 3 else [(where, 0, cut), (where + 1, cut, cut)])
        return blocks(
            jnp.stack(index).astype(jnp.int32),
            weights,
            own,
            others[side],
            [xs[op] for op in ops],
            layout,
            side,
            scale,
            given,
            final,
        )

    parts_a = run(0, (3,), run(0, (0, 1, 2), None, False), True)
    parts_b = run(1, (0, 1, 2, 3), None, True)
    resting, parts_b[0] = tie(resting, parts_b[0])
    resting = resting + send(resting, core_hop)
    grads = [ring(parts_a), ring(parts_b)]

    step_float = step_count[0].astype(jnp.float32)
    corr_first = 1.0 - jnp.exp(step_float * math.log(beta_first))
    corr_second = 1.0 - jnp.exp(step_float * math.log(beta_second))

    def update(gradient, first, second):
        first_new = beta_first * first + (1.0 - beta_first) * gradient
        second_new = beta_second * second + (1.0 - beta_second) * gradient * gradient
        return first_new / corr_first / (jnp.sqrt(second_new / corr_second) + adam_eps)

    changes = []
    for k, at in enumerate(sides):
        change = jnp.concatenate(
            [
                update(grads[k][:, :side], moment_gate[0][:, at], second_gate[0][:, at]),
                update(grads[k][:, side:], moment_up[0][:, at], second_up[0][:, at]),
            ],
            axis=1,
        )
        changes.append(change + send(change, core_hop))

    def apply(outer, velocity, fixed, change):
        mean_delta = (fixed + inner_rate * change) / islands
        velocity_new = outer_momentum * velocity + mean_delta
        return outer - outer_rate * (mean_delta + outer_momentum * velocity_new), velocity_new

    change_gate = jnp.concatenate([change[:, :side] for change in changes], axis=1)
    change_up = jnp.concatenate([change[:, side:] for change in changes], axis=1)
    out_gate, vel_gate = apply(outer_gate, velocity_gate, resting[:, :cols], change_gate)
    out_up, vel_up = apply(outer_up, velocity_up, resting[:, cols:], change_up)
    return (out_gate, out_up, vel_gate, vel_up)


def solution(mesh):
    split = Mesh(mesh.devices.reshape(2, NY, NL, NX, NH), AXES)
    tensor = ("y", "low", "x")
    state = P("core", "high", tensor)
    param = P("high", tensor)
    return jax.shard_map(
        shards,
        mesh=split,
        in_specs=(
            P(("core", "high"), tensor, None),
            P(("core", "high"), None, tensor),
            *[state] * 6,
            *[param] * 4,
            P(),
        ),
        out_specs=(param,) * 4,
        check_vma=False,
    )
```

```python
import functools
import math

import jax
import jax.numpy as jnp
from jax import lax
from jax.experimental import pallas as pl
from jax.experimental.pallas import tpu as pltpu
from jax.sharding import Mesh
from jax.sharding import PartitionSpec as P

beta_first = 0.9
beta_second = 0.95
adam_eps = 1e-08
inner_rate = 0.03
decay_rate = 0.1
outer_momentum = 0.9
outer_rate = 0.7

AXES = ("core", "y", "low", "x", "high")
NY, NL, NX, NH = 4, 2, 4, 4
NZ = NL * NH


def route(target):
    pairs = []
    for c in range(2):
        for y in range(NY):
            for l in range(NL):
                for x in range(NX):
                    for h in range(NH):
                        dc, dy, dx, dz = target(c, y, x, h * NL + l)
                        dh, dl = dz % NZ // NL, dz % NL
                        src = (((c * NY + y) * NL + l) * NX + x) * NH + h
                        dst = (((dc * NY + dy % NY) * NL + dl) * NX + dx % NX) * NH + dh
                        pairs.append((src, dst))
    return pairs


def send(block, target):
    return lax.ppermute(block, AXES, route(target))


def first_hop(step):
    return lambda c, y, x, z: (c, y, x + step, z) if c == 0 else (c, y + step, x, z)


def second_hop(step):
    return lambda c, y, x, z: (c, y + step, x, z) if c == 0 else (c, y, x + step, z)


def z_hop(step):
    return lambda c, y, x, z: (c, y, x, z + step)


def low_hop(c, y, x, z):
    return c, y, x, z ^ 1


def core_hop(c, y, x, z):
    return 1 - c, y, x, z


def block_kernel(layout, side, scale, given, final, *refs):
    index_ref, own_ref, other_ref, refs = *refs[:3], refs[3:]
    weight_refs, refs = refs[:NZ], refs[NZ:]
    n_x = 1 + max(op for piece in layout for op, _, _ in piece)
    x_refs, refs = refs[:n_x], refs[n_x:]
    if given:
        given_ref, refs = refs[0], refs[1:]
    if final:
        outs, refs = refs[:NZ], refs[NZ:]
    total, xbuf, gbuf, wbuf, pbuf, dbuf, xsem, gsem, wsem, tsem = refs
    n_pieces = len(layout)
    rows = pbuf.shape[0]
    feats = wbuf.shape[0]
    shard = feats // NH
    pair = wbuf.shape[1] // 2
    cols = pair // 2
    tok = gbuf.shape[1]
    per = rows // tok
    spots = n_pieces * per

    for k, ref in enumerate(weight_refs):
        at = pl.multiple_of(index_ref[2 * spots + k] * shard, 16)
        pltpu.make_async_copy(
            ref.at[:, pl.ds(side * pair, pair)],
            wbuf.at[pl.ds(at, shard), pl.ds(k % 2 * pair, pair)],
            wsem,
        ).start()
    for k in range(n_pieces):
        for op, first, count in layout[k]:
            pltpu.make_async_copy(
                x_refs[op], xbuf.at[pl.ds(k * rows + first, count)], xsem.at[k]
            ).start()
        for spot in range(k * per, (k + 1) * per):
            pltpu.make_async_copy(
                own_ref.at[index_ref[spot], :, pl.ds(side * cols, cols)],
                gbuf.at[spot, :, :cols],
                gsem.at[k],
            ).start()
            pltpu.make_async_copy(
                other_ref.at[index_ref[spots + spot]], gbuf.at[spot, :, cols:], gsem.at[k]
            ).start()
    if given:
        pltpu.make_async_copy(given_ref, total, tsem).start()
    pltpu.make_async_copy(wbuf, wbuf, wsem).wait()

    def forward(k, carry):
        at = pl.ds(pl.multiple_of(k * rows, 16), rows)
        pltpu.make_async_copy(xbuf.at[at], xbuf.at[at], xsem.at[k]).wait()
        mine = gbuf.at[pl.ds(k * per, per)]
        pltpu.make_async_copy(mine, mine, gsem.at[k]).wait()
        pbuf[...] = jnp.dot(xbuf[at, :], wbuf[...], preferred_element_type=jnp.float32)
        for q in range(per):
            for part in range(2):
                first = part * pair
                gate = pbuf[pl.ds(q * tok, tok), first : first + cols] * scale
                upval = pbuf[pl.ds(q * tok, tok), first + cols : first + pair] * scale
                s = jax.nn.sigmoid(gate)
                cot = gbuf[k * per + q, :, part * cols : (part + 1) * cols]
                cs = cot.astype(jnp.float32) * s
                to = pl.ds(pl.multiple_of(k * rows + q * tok, 16), tok)
                dgate = cs * upval * (1.0 + gate * (1.0 - s))
                dbuf[to, first : first + cols] = dgate.astype(jnp.bfloat16)
                dbuf[to, first + cols : first + pair] = (cs * gate).astype(jnp.bfloat16)
        return carry

    lax.fori_loop(0, n_pieces, forward, 0)
    if given:
        pltpu.make_async_copy(given_ref, total, tsem).wait()
    step = 256
    for j in range(0, feats, step):
        grad = lax.dot_general(
            xbuf[:, j : j + step],
            dbuf[...],
            (((0,), (0,)), ((), ())),
            preferred_element_type=jnp.float32,
        )
        for part in range(2):
            half = grad[:, part * pair : (part + 1) * pair]
            if given:
                half = half + total[part, pl.ds(j, step), :]
            total[part, pl.ds(j, step), :] = half
    if final:
        for k, out in enumerate(outs):
            at = pl.multiple_of(index_ref[2 * spots + k] * shard, 16)
            out[...] = (total[k % 2, pl.ds(at, shard), :] * scale).astype(jnp.bfloat16)


def blocks(index, weights, own, other, xs, layout, side, scale, given=None, final=True):
    feats, pair = weights[0].shape[0] * NH, weights[0].shape[1] // 2
    tok = own.shape[1]
    per = 4
    rows = per * tok
    n = len(layout)
    hbm = pl.BlockSpec(memory_space=pl.ANY)
    vmem = pl.BlockSpec(memory_space=pltpu.VMEM)
    operands = [index, own, other, *weights, *xs]
    if given is not None:
        operands.append(given)
    total = (2, feats, pair)
    if final:
        out_shape = [jax.ShapeDtypeStruct((feats // NH, pair), jnp.bfloat16)] * NZ
    else:
        out_shape = [jax.ShapeDtypeStruct(total, jnp.float32)]
    out = pl.pallas_call(
        functools.partial(block_kernel, layout, side, scale, given is not None, final),
        out_shape=out_shape,
        in_specs=[pl.BlockSpec(memory_space=pltpu.SMEM)] + [hbm] * (len(operands) - 1),
        out_specs=[vmem] * len(out_shape),
        scratch_shapes=([pltpu.VMEM(total, jnp.float32)] if final else [])
        + [
            pltpu.VMEM((n * rows, feats), jnp.bfloat16),
            pltpu.VMEM((n * per, tok, pair), jnp.bfloat16),
            pltpu.VMEM((feats, 2 * pair), jnp.bfloat16),
            pltpu.VMEM((rows, 2 * pair), jnp.float32),
            pltpu.VMEM((n * rows, 2 * pair), jnp.bfloat16),
            pltpu.SemaphoreType.DMA((n,)),
            pltpu.SemaphoreType.DMA((n,)),
            pltpu.SemaphoreType.DMA,
            pltpu.SemaphoreType.DMA,
        ],
        cost_estimate=pl.CostEstimate(
            flops=16 * n * rows * feats * pair, bytes_accessed=n * rows * feats * 2, transcendentals=0
        ),
        compiler_params=pltpu.CompilerParams(vmem_limit_bytes=36 * 1024 * 1024),
    )(*operands)
    return list(out) if final else out[0]


def lower_kernel(gate_ref, up_ref, out_ref):
    side = gate_ref.shape[1] // 2
    for k in range(2):
        at = slice(k * side, (k + 1) * side)
        out_ref[:, 2 * k * side : (2 * k + 1) * side] = gate_ref[:, at].astype(jnp.bfloat16)
        out_ref[:, (2 * k + 1) * side : (2 * k + 2) * side] = up_ref[:, at].astype(jnp.bfloat16)


def lower(gate, up):
    vmem = pl.BlockSpec(memory_space=pltpu.VMEM)
    return pl.pallas_call(
        lower_kernel,
        out_shape=jax.ShapeDtypeStruct((gate.shape[0], 2 * gate.shape[1]), jnp.bfloat16),
        in_specs=[vmem] * 2,
        out_specs=vmem,
        cost_estimate=pl.CostEstimate(flops=0, bytes_accessed=10 * gate.size, transcendentals=0),
        compiler_params=pltpu.CompilerParams(vmem_limit_bytes=36 * 1024 * 1024),
    )(gate, up)


def pick_kernel(first_ref, second_ref, top, bottom, sems):
    cut = top.shape[0]
    copies = [
        pltpu.make_async_copy(first_ref.at[pl.ds(0, cut)], top, sems.at[0]),
        pltpu.make_async_copy(second_ref.at[pl.ds(cut, cut)], bottom, sems.at[1]),
    ]
    for copy in copies:
        copy.start()
    for copy in copies:
        copy.wait()


def pick(first, second):
    half = jax.ShapeDtypeStruct((first.shape[0] // 2, first.shape[1]), first.dtype)
    return pl.pallas_call(
        pick_kernel,
        out_shape=[half, half],
        in_specs=[pl.BlockSpec(memory_space=pl.ANY)] * 2,
        out_specs=[pl.BlockSpec(memory_space=pltpu.VMEM)] * 2,
        scratch_shapes=[pltpu.SemaphoreType.DMA((2,))],
        cost_estimate=pl.CostEstimate(
            flops=0, bytes_accessed=4 * first.size, transcendentals=0
        ),
        compiler_params=pltpu.CompilerParams(vmem_limit_bytes=36 * 1024 * 1024),
    )(first, second)


def tie(*arrays):
    return lax.optimization_barrier(arrays)


def rest(outer, param):
    return outer - (1.0 - inner_rate * decay_rate) * param


def plus(a, *others):
    total = a.astype(jnp.float32)
    for b in others:
        total = total + b.astype(jnp.float32)
    return total


def ring(parts):
    low = jnp.bfloat16
    half = parts[0].shape[0] // 2
    up = send(parts[4][:half], z_hop(1))
    down = send(parts[4][half:], z_hop(-1))
    up = jnp.concatenate([plus(parts[3][:half], up).astype(low), parts[3][half:]], axis=0)
    down = jnp.concatenate([parts[5][:half], plus(parts[5][half:], down).astype(low)], axis=0)
    up = send(up, z_hop(1))
    down = send(down, z_hop(-1))
    up = send(plus(parts[2], up).astype(low), z_hop(1))
    down = send(plus(parts[6], down).astype(low), z_hop(-1))
    up = send(plus(parts[1], up).astype(low), z_hop(1))
    down = send(plus(parts[7], down).astype(low), z_hop(-1))
    return plus(parts[0], up, down)


def shards(
    tokens,
    hidden_cot,
    inner_gate,
    inner_up,
    moment_gate,
    moment_up,
    second_gate,
    second_up,
    outer_gate,
    outer_up,
    velocity_gate,
    velocity_up,
    step_count,
):
    islands = float(lax.axis_size("core"))
    scale = tokens.shape[2] ** (-0.5)
    core, y, low, x, high = (lax.axis_index(name) for name in AXES)
    tok = tokens.shape[1]
    cols = inner_gate.shape[2]
    side = cols // 2
    sides = [slice(0, side), slice(side, cols)]

    local = lower(inner_gate[0], inner_up[0])
    own = hidden_cot[0].reshape(NY, NL, NX * tok, cols)
    other = lax.dynamic_index_in_dim(own, 1 - low, 1, keepdims=False)
    own = own.reshape(NY * NL * NX, tok, cols)
    mine = tokens[0]

    before = send(mine, first_hop(1))
    after = send(mine, first_hop(-1))
    far = send(mine, first_hop(2))
    up1 = send(local, z_hop(1))
    down1 = send(local, z_hop(-1))
    before, after, far, up1, down1 = tie(before, after, far, up1, down1)

    line = jnp.concatenate([mine, before, after, far], axis=0)
    line_before = send(line, second_hop(1))
    line_after = send(line, second_hop(-1))
    up2 = send(up1, z_hop(1))
    down2 = send(down1, z_hop(-1))
    up3 = send(up2, z_hop(1))
    down3 = send(down2, z_hop(-1))
    others = [
        send(other[..., at], low_hop).reshape(NY * NX, tok, side) for at in sides
    ]

    cut = 2 * tok
    top, bottom = pick(line_before, line_after)
    last_a = send(top, second_hop(1))
    last_b = send(bottom, second_hop(-1))
    opposite = send(jnp.where(low == 1, up3, down3), lambda c, y, x, z: (c, y, x, z - 1 + z % 2 * 2))
    weights = [local, down1, down2, down3, opposite, up3, up2, up1]

    own_at, other_at = [], []
    for across in (0, -1, 1, 2):
        for along in (0, -1, 1, 2):
            sy = jnp.where(core == 0, y + across, y + along) % NY
            sx = jnp.where(core == 0, x + along, x + across) % NX
            own_at.append((sy * NL + low) * NX + sx)
            other_at.append(sy * NX + sx)
    z = high * NL + low
    feature_at = [(z + k) % NZ // NL for k in range(NZ)]
    xs = [line, line_before, line_after, last_a, last_b]

    def run(side, bundles, given, final):
        spots = [spot for k in bundles for spot in range(4 * k, 4 * k + 4)]
        index = [own_at[k] for k in spots] + [other_at[k] for k in spots] + feature_at
        ops = [op for k in bundles for op in ((k,) if k < 3 else (3, 4))]
        layout = []
        for k in bundles:
            where = ops.index(k)
            layout.append([(where, 0, 4 * tok)] if k < 3 else [(where, 0, cut), (where + 1, cut, cut)])
        return blocks(
            jnp.stack(index).astype(jnp.int32),
            weights,
            own,
            others[side],
            [xs[op] for op in ops],
            layout,
            side,
            scale,
            given,
            final,
        )

    parts_a = run(0, (3,), run(0, (0, 1, 2), None, False), True)
    others[1], *parts_a = tie(others[1], *parts_a)
    parts_b = run(1, (0, 1, 2, 3), None, True)
    resting = jnp.concatenate(
        [rest(outer_gate, inner_gate[0]), rest(outer_up, inner_up[0])], axis=1
    )
    resting, parts_b[0] = tie(resting, parts_b[0])
    resting = resting + send(resting, core_hop)
    grads = [ring(parts_a), ring(parts_b)]

    step_float = step_count[0].astype(jnp.float32)
    corr_first = 1.0 - jnp.exp(step_float * math.log(beta_first))
    corr_second = 1.0 - jnp.exp(step_float * math.log(beta_second))

    def update(gradient, first, second):
        first_new = beta_first * first + (1.0 - beta_first) * gradient
        second_new = beta_second * second + (1.0 - beta_second) * gradient * gradient
        return first_new / corr_first / (jnp.sqrt(second_new / corr_second) + adam_eps)

    changes = []
    for k, at in enumerate(sides):
        change = jnp.concatenate(
            [
                update(grads[k][:, :side], moment_gate[0][:, at], second_gate[0][:, at]),
                update(grads[k][:, side:], moment_up[0][:, at], second_up[0][:, at]),
            ],
            axis=1,
        )
        changes.append(change + send(change, core_hop))

    def apply(outer, velocity, fixed, change):
        mean_delta = (fixed + inner_rate * change) / islands
        velocity_new = outer_momentum * velocity + mean_delta
        return outer - outer_rate * (mean_delta + outer_momentum * velocity_new), velocity_new

    change_gate = jnp.concatenate([change[:, :side] for change in changes], axis=1)
    change_up = jnp.concatenate([change[:, side:] for change in changes], axis=1)
    out_gate, vel_gate = apply(outer_gate, velocity_gate, resting[:, :cols], change_gate)
    out_up, vel_up = apply(outer_up, velocity_up, resting[:, cols:], change_up)
    return (out_gate, out_up, vel_gate, vel_up)


def solution(mesh):
    split = Mesh(mesh.devices.reshape(2, NY, NL, NX, NH), AXES)
    tensor = ("y", "low", "x")
    state = P("core", "high", tensor)
    param = P("high", tensor)
    return jax.shard_map(
        shards,
        mesh=split,
        in_specs=(
            P(("core", "high"), tensor, None),
            P(("core", "high"), None, tensor),
            *[state] * 6,
            *[param] * 4,
            P(),
        ),
        out_specs=(param,) * 4,
        check_vma=False,
    )
```

```python
import functools
import math

import jax
import jax.numpy as jnp
from jax import lax
from jax.experimental import pallas as pl
from jax.experimental.pallas import tpu as pltpu
from jax.sharding import Mesh
from jax.sharding import PartitionSpec as P

beta_first = 0.9
beta_second = 0.95
adam_eps = 1e-08
inner_rate = 0.03
decay_rate = 0.1
outer_momentum = 0.9
outer_rate = 0.7

AXES = ("core", "y", "low", "x", "high")
NY, NL, NX, NH = 4, 2, 4, 4
NZ = NL * NH
MESSAGES = (
    ((4, 0), (3, 1)),
    ((3, 0), (2, 1)),
    ((2, 0), (1, 1)),
    ((1, 0),),
    ((5, 0), (4, 1)),
    ((6, 0), (5, 1)),
    ((7, 0), (6, 1)),
    ((7, 1),),
    ((0, 0), (0, 1)),
)


def route(target):
    pairs = []
    for c in range(2):
        for y in range(NY):
            for l in range(NL):
                for x in range(NX):
                    for h in range(NH):
                        dc, dy, dx, dz = target(c, y, x, h * NL + l)
                        dh, dl = dz % NZ // NL, dz % NL
                        src = (((c * NY + y) * NL + l) * NX + x) * NH + h
                        dst = (((dc * NY + dy % NY) * NL + dl) * NX + dx % NX) * NH + dh
                        pairs.append((src, dst))
    return pairs


def send(block, target):
    return lax.ppermute(block, AXES, route(target))


def first_hop(step):
    return lambda c, y, x, z: (c, y, x + step, z) if c == 0 else (c, y + step, x, z)


def second_hop(step):
    return lambda c, y, x, z: (c, y + step, x, z) if c == 0 else (c, y, x + step, z)


def z_hop(step):
    return lambda c, y, x, z: (c, y, x, z + step)


def low_hop(c, y, x, z):
    return c, y, x, z ^ 1


def core_hop(c, y, x, z):
    return 1 - c, y, x, z


def block_kernel(layout, side, scale, given, final, *refs):
    index_ref, own_ref, other_ref, refs = *refs[:3], refs[3:]
    weight_refs, refs = refs[:NZ], refs[NZ:]
    n_x = 1 + max(op for piece in layout for op, _, _ in piece)
    x_refs, refs = refs[:n_x], refs[n_x:]
    if given:
        given_ref, refs = refs[0], refs[1:]
    if final:
        outs, refs = refs[: len(MESSAGES)], refs[len(MESSAGES) :]
    total, xbuf, gbuf, wbuf, pbuf, dbuf, xsem, gsem, wsem, tsem = refs
    n_pieces = len(layout)
    rows = pbuf.shape[0]
    feats = wbuf.shape[0]
    shard = feats // NH
    pair = wbuf.shape[1] // 2
    cols = pair // 2
    tok = gbuf.shape[1]
    per = rows // tok
    spots = n_pieces * per

    for k, ref in enumerate(weight_refs):
        at = pl.multiple_of(index_ref[2 * spots + k] * shard, 16)
        pltpu.make_async_copy(
            ref.at[:, pl.ds(side * pair, pair)],
            wbuf.at[pl.ds(at, shard), pl.ds(k % 2 * pair, pair)],
            wsem,
        ).start()
    for k in range(n_pieces):
        for op, first, count in layout[k]:
            pltpu.make_async_copy(
                x_refs[op], xbuf.at[pl.ds(k * rows + first, count)], xsem.at[k]
            ).start()
        for spot in range(k * per, (k + 1) * per):
            pltpu.make_async_copy(
                own_ref.at[index_ref[spot], :, pl.ds(side * cols, cols)],
                gbuf.at[spot, :, :cols],
                gsem.at[k],
            ).start()
            pltpu.make_async_copy(
                other_ref.at[index_ref[spots + spot]], gbuf.at[spot, :, cols:], gsem.at[k]
            ).start()
    if given:
        pltpu.make_async_copy(given_ref, total, tsem).start()
    pltpu.make_async_copy(wbuf, wbuf, wsem).wait()

    def forward(k, carry):
        at = pl.ds(pl.multiple_of(k * rows, 16), rows)
        pltpu.make_async_copy(xbuf.at[at], xbuf.at[at], xsem.at[k]).wait()
        mine = gbuf.at[pl.ds(k * per, per)]
        pltpu.make_async_copy(mine, mine, gsem.at[k]).wait()
        pbuf[...] = jnp.dot(xbuf[at, :], wbuf[...], preferred_element_type=jnp.float32)
        for q in range(per):
            for part in range(2):
                first = part * pair
                gate = pbuf[pl.ds(q * tok, tok), first : first + cols] * scale
                upval = pbuf[pl.ds(q * tok, tok), first + cols : first + pair] * scale
                s = jax.nn.sigmoid(gate)
                cot = gbuf[k * per + q, :, part * cols : (part + 1) * cols]
                cs = cot.astype(jnp.float32) * s
                to = pl.ds(pl.multiple_of(k * rows + q * tok, 16), tok)
                dgate = cs * upval * (1.0 + gate * (1.0 - s))
                dbuf[to, first : first + cols] = dgate.astype(jnp.bfloat16)
                dbuf[to, first + cols : first + pair] = (cs * gate).astype(jnp.bfloat16)
        return carry

    lax.fori_loop(0, n_pieces, forward, 0)
    if given:
        pltpu.make_async_copy(given_ref, total, tsem).wait()
    step = 256
    for j in range(0, feats, step):
        grad = lax.dot_general(
            xbuf[:, j : j + step],
            dbuf[...],
            (((0,), (0,)), ((), ())),
            preferred_element_type=jnp.float32,
        )
        for part in range(2):
            half = grad[:, part * pair : (part + 1) * pair]
            if given:
                half = half + total[part, pl.ds(j, step), :]
            total[part, pl.ds(j, step), :] = half
    if final:
        half = shard // 2
        for message, out in zip(MESSAGES, outs):
            for spot, (k, part) in enumerate(message):
                at = pl.multiple_of(index_ref[2 * spots + k] * shard + part * half, 16)
                rounded = (total[k % 2, pl.ds(at, half), :] * scale).astype(jnp.bfloat16)
                out[pl.ds(spot * half, half), :] = rounded


def blocks(index, weights, own, other, xs, layout, side, scale, given=None, final=True):
    feats, pair = weights[0].shape[0] * NH, weights[0].shape[1] // 2
    tok = own.shape[1]
    per = 4
    rows = per * tok
    n = len(layout)
    hbm = pl.BlockSpec(memory_space=pl.ANY)
    vmem = pl.BlockSpec(memory_space=pltpu.VMEM)
    operands = [index, own, other, *weights, *xs]
    if given is not None:
        operands.append(given)
    total = (2, feats, pair)
    if final:
        half = feats // NH // 2
        out_shape = [
            jax.ShapeDtypeStruct((len(message) * half, pair), jnp.bfloat16) for message in MESSAGES
        ]
    else:
        out_shape = [jax.ShapeDtypeStruct(total, jnp.float32)]
    out = pl.pallas_call(
        functools.partial(block_kernel, layout, side, scale, given is not None, final),
        out_shape=out_shape,
        in_specs=[pl.BlockSpec(memory_space=pltpu.SMEM)] + [hbm] * (len(operands) - 1),
        out_specs=[vmem] * len(out_shape),
        scratch_shapes=([pltpu.VMEM(total, jnp.float32)] if final else [])
        + [
            pltpu.VMEM((n * rows, feats), jnp.bfloat16),
            pltpu.VMEM((n * per, tok, pair), jnp.bfloat16),
            pltpu.VMEM((feats, 2 * pair), jnp.bfloat16),
            pltpu.VMEM((rows, 2 * pair), jnp.float32),
            pltpu.VMEM((n * rows, 2 * pair), jnp.bfloat16),
            pltpu.SemaphoreType.DMA((n,)),
            pltpu.SemaphoreType.DMA((n,)),
            pltpu.SemaphoreType.DMA,
            pltpu.SemaphoreType.DMA,
        ],
        cost_estimate=pl.CostEstimate(
            flops=16 * n * rows * feats * pair, bytes_accessed=n * rows * feats * 2, transcendentals=0
        ),
        compiler_params=pltpu.CompilerParams(vmem_limit_bytes=36 * 1024 * 1024),
    )(*operands)
    return list(out) if final else out[0]


def lower_kernel(gate_ref, up_ref, out_ref):
    side = gate_ref.shape[1] // 2
    for k in range(2):
        at = slice(k * side, (k + 1) * side)
        out_ref[:, 2 * k * side : (2 * k + 1) * side] = gate_ref[:, at].astype(jnp.bfloat16)
        out_ref[:, (2 * k + 1) * side : (2 * k + 2) * side] = up_ref[:, at].astype(jnp.bfloat16)


def lower(gate, up):
    vmem = pl.BlockSpec(memory_space=pltpu.VMEM)
    return pl.pallas_call(
        lower_kernel,
        out_shape=jax.ShapeDtypeStruct((gate.shape[0], 2 * gate.shape[1]), jnp.bfloat16),
        in_specs=[vmem] * 2,
        out_specs=vmem,
        cost_estimate=pl.CostEstimate(flops=0, bytes_accessed=10 * gate.size, transcendentals=0),
        compiler_params=pltpu.CompilerParams(vmem_limit_bytes=36 * 1024 * 1024),
    )(gate, up)


def pick_kernel(first_ref, second_ref, top, bottom, sems):
    cut = top.shape[0]
    copies = [
        pltpu.make_async_copy(first_ref.at[pl.ds(0, cut)], top, sems.at[0]),
        pltpu.make_async_copy(second_ref.at[pl.ds(cut, cut)], bottom, sems.at[1]),
    ]
    for copy in copies:
        copy.start()
    for copy in copies:
        copy.wait()


def pick(first, second):
    half = jax.ShapeDtypeStruct((first.shape[0] // 2, first.shape[1]), first.dtype)
    return pl.pallas_call(
        pick_kernel,
        out_shape=[half, half],
        in_specs=[pl.BlockSpec(memory_space=pl.ANY)] * 2,
        out_specs=[pl.BlockSpec(memory_space=pltpu.VMEM)] * 2,
        scratch_shapes=[pltpu.SemaphoreType.DMA((2,))],
        cost_estimate=pl.CostEstimate(
            flops=0, bytes_accessed=4 * first.size, transcendentals=0
        ),
        compiler_params=pltpu.CompilerParams(vmem_limit_bytes=36 * 1024 * 1024),
    )(first, second)


def tie(*arrays):
    return lax.optimization_barrier(arrays)


def rest(outer, param):
    return outer - (1.0 - inner_rate * decay_rate) * param


def plus(a, *others):
    total = a.astype(jnp.float32)
    for b in others:
        total = total + b.astype(jnp.float32)
    return total


def ring_first(parts):
    return send(parts[0], z_hop(1)), send(parts[4], z_hop(-1))


def ring(parts, up, down):
    low = jnp.bfloat16
    half = parts[3].shape[0]
    for k in range(1, 3):
        up = send(plus(parts[k], up).astype(low), z_hop(1))
        down = send(plus(parts[4 + k], down).astype(low), z_hop(-1))
    last_up = send(plus(parts[3], up[:half]).astype(low), z_hop(1))
    last_down = send(plus(parts[7], down[half:]).astype(low), z_hop(-1))
    own = parts[8]
    top = plus(own[:half], last_up, down[:half])
    bottom = plus(own[half:], up[half:], last_down)
    return jnp.concatenate([top, bottom], axis=0)


def shards(
    tokens,
    hidden_cot,
    inner_gate,
    inner_up,
    moment_gate,
    moment_up,
    second_gate,
    second_up,
    outer_gate,
    outer_up,
    velocity_gate,
    velocity_up,
    step_count,
):
    islands = float(lax.axis_size("core"))
    scale = tokens.shape[2] ** (-0.5)
    core, y, low, x, high = (lax.axis_index(name) for name in AXES)
    tok = tokens.shape[1]
    cols = inner_gate.shape[2]
    side = cols // 2
    sides = [slice(0, side), slice(side, cols)]

    local = lower(inner_gate[0], inner_up[0])
    own = hidden_cot[0].reshape(NY, NL, NX * tok, cols)
    other = lax.dynamic_index_in_dim(own, 1 - low, 1, keepdims=False)
    own = own.reshape(NY * NL * NX, tok, cols)
    mine = tokens[0]

    before = send(mine, first_hop(1))
    after = send(mine, first_hop(-1))
    far = send(mine, first_hop(2))
    up1 = send(local, z_hop(1))
    down1 = send(local, z_hop(-1))

    line = jnp.concatenate([mine, before, after, far], axis=0)
    line_before = send(line, second_hop(1))
    line_after = send(line, second_hop(-1))
    up2 = send(up1, z_hop(1))
    down2 = send(down1, z_hop(-1))
    up3 = send(up2, z_hop(1))
    down3 = send(down2, z_hop(-1))
    others = [
        send(other[..., at], low_hop).reshape(NY * NX, tok, side) for at in sides
    ]

    cut = 2 * tok
    top, bottom = pick(line_before, line_after)
    last_a = send(top, second_hop(1))
    last_b = send(bottom, second_hop(-1))
    opposite = send(jnp.where(low == 1, up3, down3), lambda c, y, x, z: (c, y, x, z - 1 + z % 2 * 2))
    weights = [local, down1, down2, down3, opposite, up3, up2, up1]

    own_at, other_at = [], []
    for across in (0, -1, 1, 2):
        for along in (0, -1, 1, 2):
            sy = jnp.where(core == 0, y + across, y + along) % NY
            sx = jnp.where(core == 0, x + along, x + across) % NX
            own_at.append((sy * NL + low) * NX + sx)
            other_at.append(sy * NX + sx)
    z = high * NL + low
    feature_at = [(z + k) % NZ // NL for k in range(NZ)]
    xs = [line, line_before, line_after, last_a, last_b]

    def run(side, bundles, given, final):
        spots = [spot for k in bundles for spot in range(4 * k, 4 * k + 4)]
        index = [own_at[k] for k in spots] + [other_at[k] for k in spots] + feature_at
        ops = [op for k in bundles for op in ((k,) if k < 3 else (3, 4))]
        layout = []
        for k in bundles:
            where = ops.index(k)
            layout.append([(where, 0, 4 * tok)] if k < 3 else [(where, 0, cut), (where + 1, cut, cut)])
        return blocks(
            jnp.stack(index).astype(jnp.int32),
            weights,
            own,
            others[side],
            [xs[op] for op in ops],
            layout,
            side,
            scale,
            given,
            final,
        )

    parts_a = run(0, (3,), run(0, (0, 1, 2), None, False), True)
    others[1], *parts_a = tie(others[1], *parts_a)
    parts_b = run(1, (0, 1, 2, 3), None, True)
    resting = jnp.concatenate(
        [rest(outer_gate, inner_gate[0]), rest(outer_up, inner_up[0])], axis=1
    )
    resting, parts_b[8] = tie(resting, parts_b[8])
    resting = resting + send(resting, core_hop)
    up_a, down_a, parts_b[0], parts_b[4] = tie(*ring_first(parts_a), parts_b[0], parts_b[4])
    grads = [ring(parts_a, up_a, down_a), ring(parts_b, *ring_first(parts_b))]

    step_float = step_count[0].astype(jnp.float32)
    corr_first = 1.0 - jnp.exp(step_float * math.log(beta_first))
    corr_second = 1.0 - jnp.exp(step_float * math.log(beta_second))

    def update(gradient, first, second):
        first_new = beta_first * first + (1.0 - beta_first) * gradient
        second_new = beta_second * second + (1.0 - beta_second) * gradient * gradient
        return first_new / corr_first / (jnp.sqrt(second_new / corr_second) + adam_eps)

    changes = []
    for k, at in enumerate(sides):
        change = jnp.concatenate(
            [
                update(grads[k][:, :side], moment_gate[0][:, at], second_gate[0][:, at]),
                update(grads[k][:, side:], moment_up[0][:, at], second_up[0][:, at]),
            ],
            axis=1,
        )
        changes.append(change + send(change, core_hop))

    def apply(outer, velocity, fixed, change):
        mean_delta = (fixed + inner_rate * change) / islands
        velocity_new = outer_momentum * velocity + mean_delta
        return outer - outer_rate * (mean_delta + outer_momentum * velocity_new), velocity_new

    change_gate = jnp.concatenate([change[:, :side] for change in changes], axis=1)
    change_up = jnp.concatenate([change[:, side:] for change in changes], axis=1)
    out_gate, vel_gate = apply(outer_gate, velocity_gate, resting[:, :cols], change_gate)
    out_up, vel_up = apply(outer_up, velocity_up, resting[:, cols:], change_up)
    return (out_gate, out_up, vel_gate, vel_up)


def solution(mesh):
    split = Mesh(mesh.devices.reshape(2, NY, NL, NX, NH), AXES)
    tensor = ("y", "low", "x")
    state = P("core", "high", tensor)
    param = P("high", tensor)
    return jax.shard_map(
        shards,
        mesh=split,
        in_specs=(
            P(("core", "high"), tensor, None),
            P(("core", "high"), None, tensor),
            *[state] * 6,
            *[param] * 4,
            P(),
        ),
        out_specs=(param,) * 4,
        check_vma=False,
    )
```
